32 devices in a mesh: gx: 8 (over z, core), gy: 4 (over y, x).
Axes of the slice: x: 2, y: 2, z: 4, core: 2. Of those that a mesh axis runs over, the one named last changes fastest.
Arguments:
- payload: float32 [4, 524288], P(None, ('gx', 'gy'))
- cells: int32 [3, 524288], P(None, ('gx', 'gy')), may hold values from 0 to 127, as said below
- counts: int32 [32, 9], P(('gx', 'gy')), may hold values from 128 to 12596, as said below
Outputs:
- scalar_field: float32 [8, 128, 512], P(None, 'gx', 'gy')
- momentum: float32 [3, 8, 128, 512], P(None, None, 'gx', 'gy')
The draws below stay inside these ranges and needn't reach their ends.
Inputs may be any that keep to these rules, and one draw needn't show every extreme that they name: Rows of a tile are grouped by direction in the order of counts' columns. A face direction holds at most 2048 rows of a tile and a corner direction at most 512; each of these bounds is reached in some tile. A row of counts sums to 16384. cells[0] is below 8, cells[1] below 16, cells[2] below 128. A particle moving +x lands in x layers 0 to 1 of its destination tile, one moving -x in layers 14 to 15; likewise +y in y layers 0 to 15 and -y in 112 to 127; corner directions are bound in both; otherwise any cell.
All inputs are finite; a program needn't handle non-finite values.
Results may differ from the reference program's by a relative error of at most 0.000054.
Values sent between devices are 32-bit elements; how exact they have to be, the bound alone decides.
A program may use at most 64 MiB of HBM per device.

```python
import jax
import jax.numpy as jnp

CX = 16
CY = 128
NZ = 8
SWEEPS = 4
PART = 16384
CAP_F = 2048
CAP_D = 512
MX = 2
MY = 16
TILES = 32
PARTS_ALL = 524288
NX = 128
NY = 512
N_GX = 8
N_GY = 4


def tile_counts(key):
    base = jax.random.fold_in(key, 7)
    key_face, key_corner, key_topf, key_topc, key_low = jax.random.split(base, 5)
    low_face = 2 * CAP_F // 5
    low_corner = CAP_D // 4
    face_counts = jax.random.randint(key_face, (TILES, 4), low_face, CAP_F + 1)
    corner_counts = jax.random.randint(key_corner, (TILES, 4), low_corner, CAP_D + 1)
    low_tile = jax.random.randint(key_low, (), 0, TILES)
    top_face = (low_tile + 1 + jax.random.randint(key_topf, (4,), 0, TILES - 1)) % TILES
    top_corner = (low_tile + 1 + jax.random.randint(key_topc, (4,), 0, TILES - 1)) % TILES
    tile_rows = jnp.arange(TILES)[:, None]
    face_counts = jnp.where(tile_rows == low_tile, low_face, face_counts)
    corner_counts = jnp.where(tile_rows == low_tile, low_corner, corner_counts)
    face_counts = jnp.where(tile_rows == top_face[None, :], CAP_F, face_counts)
    corner_counts = jnp.where(tile_rows == top_corner[None, :], CAP_D, corner_counts)
    staying = PART - jnp.sum(face_counts, axis=1) - jnp.sum(corner_counts, axis=1)
    return jnp.concatenate([face_counts, corner_counts, staying[:, None]], axis=1).astype(jnp.int32)


def draw_counts(key, part):
    return tile_counts(key)


def draw_cells(key, part):
    counts = tile_counts(key)
    limits = jnp.cumsum(counts, axis=1)
    position = jnp.arange(PART, dtype=jnp.int32)
    direction = jnp.zeros((TILES, PART), jnp.int32)
    for edge in range(8):
        direction = direction + (position[None, :] >= limits[:, edge:edge + 1]).astype(jnp.int32)
    step_x = ((direction == 0) | (direction == 4) | (direction == 5)).astype(jnp.int32) - ((direction == 1) | (direction == 6) | (direction == 7)).astype(jnp.int32)
    step_y = ((direction == 2) | (direction == 4) | (direction == 6)).astype(jnp.int32) - ((direction == 3) | (direction == 5) | (direction == 7)).astype(jnp.int32)
    base = jax.random.fold_in(key, 13)
    key_i, key_j, key_k = jax.random.split(base, 3)
    raw_i = jax.random.randint(key_i, (TILES, PART), 0, 2 ** 20)
    raw_j = jax.random.randint(key_j, (TILES, PART), 0, 2 ** 20)
    depth_k = jax.random.randint(key_k, (TILES, PART), 0, NZ)
    start_i = jnp.where(step_x == -1, CX - MX, 0)
    span_i = jnp.where(step_x == 0, CX, MX)
    start_j = jnp.where(step_y == -1, CY - MY, 0)
    span_j = jnp.where(step_y == 0, CY, MY)
    place_i = start_i + raw_i % span_i
    place_j = start_j + raw_j % span_j
    return jnp.stack([depth_k.reshape(-1), place_i.reshape(-1), place_j.reshape(-1)], axis=0).astype(jnp.int32)


def draw_payload(key, part):
    key_mass, key_speed = jax.random.split(jax.random.fold_in(key, 29))
    masses = jnp.exp(jax.random.uniform(key_mass, (1, PARTS_ALL), jnp.float32, jnp.log(0.3), jnp.log(3.0)))
    speeds = jnp.clip(jax.random.normal(key_speed, (3, PARTS_ALL), jnp.float32), -4.0, 4.0)
    return jnp.concatenate([masses, speeds], axis=0).astype(jnp.float32)


def setup_inputs(seed: int = 0) -> dict:
    streams_of = jax.random.split(jax.random.key(seed), 4)
    payload = draw_payload(jax.random.fold_in(streams_of[3], 71), 0)
    cells = draw_cells(jax.random.fold_in(streams_of[3], 71), 0)
    counts = draw_counts(jax.random.fold_in(streams_of[3], 71), 0)
    return dict(payload=payload, cells=cells, counts=counts)


SCREENING = 0.5
CUBIC_TERM = 0.3
COUPLING = 1.5
SMOOTHING = 0.1
BACKGROUND = 1.0


def row_directions(counts):
    limits = jnp.cumsum(counts, axis=1)
    position = jnp.arange(PART, dtype=jnp.int32)
    direction = jnp.zeros((TILES, PART), jnp.int32)
    for edge in range(8):
        direction = direction + (position[None, :] >= limits[:, edge:edge + 1]).astype(jnp.int32)
    return direction.reshape(-1)


def direction_steps(direction):
    step_x = ((direction == 0) | (direction == 4) | (direction == 5)).astype(jnp.int32) - ((direction == 1) | (direction == 6) | (direction == 7)).astype(jnp.int32)
    step_y = ((direction == 2) | (direction == 4) | (direction == 6)).astype(jnp.int32) - ((direction == 3) | (direction == 5) | (direction == 7)).astype(jnp.int32)
    return step_x, step_y


def neighbours(field):
    stacked = jnp.pad(field, ((1, 1), (0, 0), (0, 0)))
    return stacked[2:] + stacked[:-2] + jnp.roll(field, -1, 1) + jnp.roll(field, 1, 1) + jnp.roll(field, -1, 2) + jnp.roll(field, 1, 2)


def reference(payload, cells, counts):
    direction = row_directions(counts)
    step_x, step_y = direction_steps(direction)
    tile_index = jnp.arange(PARTS_ALL, dtype=jnp.int32) // PART
    tile_x = tile_index // N_GY
    tile_y = tile_index % N_GY
    depth_k = cells[0]
    place_i = cells[1]
    place_j = cells[2]
    global_x = ((tile_x + step_x) % N_GX) * CX + place_i
    global_y = ((tile_y + step_y) % N_GY) * CY + place_j
    flat_index = (depth_k * NX + global_x) * NY + global_y
    masses = payload[0]
    density = jnp.zeros((NZ * NX * NY,), jnp.float32).at[flat_index].add(masses).reshape(NZ, NX, NY)
    moments = []
    for component in range(3):
        moments.append(jnp.zeros((NZ * NX * NY,), jnp.float32).at[flat_index].add(masses * payload[component + 1]).reshape(NZ, NX, NY))
    momentum = jnp.stack(moments, axis=0)
    smoothed = density + SMOOTHING * (neighbours(density) - 6.0 * density)
    source = COUPLING * (smoothed - BACKGROUND)
    parity = (jnp.arange(NZ, dtype=jnp.int32)[:, None, None] + jnp.arange(NX, dtype=jnp.int32)[None, :, None] + jnp.arange(NY, dtype=jnp.int32)[None, None, :]) % 2
    scalar_field = jnp.zeros((NZ, NX, NY), jnp.float32)
    for sweep_no in range(SWEEPS):
        for colour in (0, 1):
            middle = scalar_field
            residual = neighbours(middle) - 6.0 * middle - SCREENING * middle - CUBIC_TERM * middle * middle * middle - source
            slope = -6.0 - SCREENING - 3.0 * CUBIC_TERM * middle * middle
            scalar_field = jnp.where(parity == colour, middle - residual / slope, middle)
    return scalar_field, momentum
```

```python
import functools

import jax
import jax.numpy as jnp
from jax import lax
from jax.experimental import pallas as pl
from jax.experimental.pallas import tpu as pltpu
from jax.sharding import PartitionSpec as P

CX = 16
CY = 128
NZ = 8
SWEEPS = 4
MX = 2
MY = 16
HALO = 8
BLOCK = 1024
STAY = 64
LEAVE = 48

SCREENING = 0.5
CUBIC_TERM = 0.3
COUPLING = 1.5
SMOOTHING = 0.1
BACKGROUND = 1.0

MESH = pl.DeviceIdType.MESH
STEPS = ((1, 0), (-1, 0), (0, 1), (0, -1), (1, 1), (1, -1), (-1, 1), (-1, -1))


def deposit_kernel(counts, payload, cells, main, xs, ys, cs, stay_acc, leave_acc):
    part = payload.shape[1]
    limits = []
    total = jnp.int32(0)
    for e in range(8):
        total = total + counts[0, e]
        limits.append(total)
    stay_acc[...] = jnp.zeros_like(stay_acc)
    leave_acc[...] = jnp.zeros_like(leave_acc)

    def hot_rows(count, index):
        ids = lax.broadcasted_iota(jnp.int32, (count, BLOCK), 0)
        return jnp.where(ids == index, 1.0, 0.0).astype(jnp.bfloat16)

    def step(b, carry):
        start = pl.multiple_of(b * BLOCK, BLOCK)
        span = pl.ds(start, BLOCK)
        position = start + lax.broadcasted_iota(jnp.int32, (1, BLOCK), 1)
        direction = jnp.zeros((1, BLOCK), jnp.int32)
        for e in range(8):
            direction = direction + (position >= limits[e]).astype(jnp.int32)
        k = cells[0:1, span]
        i = cells[1:2, span]
        j = cells[2:3, span]
        stays = direction == 8
        chunk = k * MY + (j & (MY - 1))
        layer = i & 1
        leave_row = jnp.where(
            direction < 2, k * MX + layer, jnp.where(direction < 4, 16 + i, 28 + direction)
        )
        leave_col = jnp.where(
            direction < 2,
            direction * CY + j,
            jnp.where(direction < 4, (direction - 2) * CY, layer * CY) + chunk,
        )
        stay_row = jnp.where(stays, k * 8 + (i & 7), -1)
        leave_row = jnp.where(stays, -1, leave_row)
        col = jnp.where(stays, (i >> 3) * CY + j, leave_col)
        cols_hot = hot_rows(2 * CY, col)
        mass = payload[0:1, span]
        values = [mass] + [mass * payload[c : c + 1, span] for c in range(1, 4)]
        highs = [v.astype(jnp.bfloat16).astype(jnp.float32) for v in values]
        lows = [v - h for v, h in zip(values, highs)]
        wide = [jnp.broadcast_to(v, (16, BLOCK)).astype(jnp.bfloat16) for v in highs + lows]

        def add(acc, count, index):
            hot = hot_rows(count, index).reshape(count // 16, 16, BLOCK)
            left = jnp.concatenate(
                [(hot * w[None]).reshape(count, BLOCK) for w in wide], axis=0
            )
            acc[...] += lax.dot_general(
                left, cols_hot, (((1,), (1,)), ((), ())), preferred_element_type=jnp.float32
            )

        @pl.when(start + BLOCK > limits[7])
        def _():
            add(stay_acc, STAY, stay_row)

        @pl.when(start < limits[7])
        def _():
            add(leave_acc, LEAVE, leave_row)

        return carry

    lax.fori_loop(0, part // BLOCK, step, 0)
    for c in range(4):
        for h in range(2):
            lanes = slice(h * CY, (h + 1) * CY)
            whole = (
                stay_acc[c * STAY : (c + 1) * STAY, lanes]
                + stay_acc[(4 + c) * STAY : (5 + c) * STAY, lanes]
            )
            main[c, :, 8 * h : 8 * h + 8, :] = whole.reshape(NZ, 8, CY)
            out = (
                leave_acc[c * LEAVE : (c + 1) * LEAVE, lanes]
                + leave_acc[(4 + c) * LEAVE : (5 + c) * LEAVE, lanes]
            )
            xs[h, c] = out[0:16]
            ys[h, c] = out[16:32]
            for d in range(4):
                cs[d, 2 * c + h : 2 * c + h + 1, :] = out[32 + d : 33 + d]


def relax_kernel(
    sizes, main, xs, ys, cs, field, momentum,
    rx, ry, rc, dens, edges, hx, hy, ext, src, u,
    send1, recv1, send2, recv2,
):
    n_gx, n_gy = sizes
    me_x = lax.axis_index("gx")
    me_y = lax.axis_index("gy")

    def device(step):
        return (lax.rem(me_x + step[0] + n_gx, n_gx), lax.rem(me_y + step[1] + n_gy, n_gy))

    barrier = pltpu.get_barrier_semaphore()
    for step in STEPS:
        pl.semaphore_signal(barrier, inc=1, device_id=device(step), device_id_type=MESH)
    pl.semaphore_wait(barrier, 8)

    def remote(src_ref, dst_ref, sems, recvs, d):
        return pltpu.make_async_remote_copy(
            src_ref=src_ref, dst_ref=dst_ref, send_sem=sems.at[d], recv_sem=recvs.at[d],
            device_id=device(STEPS[d]), device_id_type=MESH,
        )

    first = []
    for d in range(8):
        if d < 2:
            pair = (xs.at[d], rx.at[d])
        elif d < 4:
            pair = (ys.at[d - 2], ry.at[d - 2])
        else:
            pair = (cs.at[d - 4], rc.at[d - 4])
        first.append(remote(pair[0], pair[1], send1, recv1, d))
    for copy in first:
        copy.start()
    lane = lax.broadcasted_iota(jnp.int32, (1, CY), 1)
    lane16 = lax.broadcasted_iota(jnp.int32, (CX, CY), 1)
    for copy in first:
        copy.wait_recv()

    def collected(c):
        sides = []
        for s in range(2):
            low = rc[s, 2 * c : 2 * c + 2, :]
            high = rc[2 + s, 2 * c : 2 * c + 2, :]
            pad = jnp.zeros((CX - 2 * MX, CY), jnp.float32)
            sides.append(ry[s, c] + jnp.concatenate([low, pad, high], axis=0))
        pad = jnp.zeros((CX - 2 * MX, CY), jnp.float32)
        out = []
        for k in range(NZ):
            left = pltpu.roll(sides[0], (CY - MY * k) % CY, axis=1)
            right = pltpu.roll(sides[1], (2 * CY - MY - MY * k) % CY, axis=1)
            extra = jnp.where(lane16 < MY, left, jnp.where(lane16 >= CY - MY, right, 0.0))
            faces = jnp.concatenate(
                [rx[0, c, 2 * k : 2 * k + 2, :], pad, rx[1, c, 2 * k : 2 * k + 2, :]], axis=0
            )
            out.append(main[c, k] + faces + extra)
        return out

    rho = collected(0)
    low_edge = jnp.zeros((CX, CY), jnp.float32)
    high_edge = jnp.zeros((CX, CY), jnp.float32)
    for k in range(NZ):
        dens[k] = rho[k]
        here = (lane16 >= MY * k) & (lane16 < MY * (k + 1))
        low_edge = jnp.where(here, pltpu.roll(rho[k], MY * k, axis=1), low_edge)
        high_edge = jnp.where(here, pltpu.roll(rho[k], (MY * (k + 1)) % CY, axis=1), high_edge)
    edges[0] = low_edge
    edges[1] = high_edge

    second = [
        (dens.at[:, 8:16, :], hx.at[0]),
        (dens.at[:, 0:8, :], hx.at[1]),
        (edges.at[1], hy.at[1, 8:24, :]),
        (edges.at[0], hy.at[0, 8:24, :]),
        (edges.at[1, 8:16, :], hy.at[1, 0:8, :]),
        (edges.at[0, 8:16, :], hy.at[0, 0:8, :]),
        (edges.at[1, 0:8, :], hy.at[1, 24:32, :]),
        (edges.at[0, 0:8, :], hy.at[0, 24:32, :]),
    ]
    second = [remote(a, b, send2, recv2, d) for d, (a, b) in enumerate(second)]
    for copy in second:
        copy.start()
    for c in range(1, 4):
        for k, layer in enumerate(collected(c)):
            momentum[c - 1, k] = layer
    for copy in second:
        copy.wait_recv()

    lane32 = lax.broadcasted_iota(jnp.int32, (32, CY), 1)
    for k in range(NZ):
        ext[k, 0:8, 0:CY] = hx[0, k]
        ext[k, 8:24, 0:CY] = dens[k]
        ext[k, 24:32, 0:CY] = hx[1, k]
        after = pltpu.roll(hy[0], (CY - MY * k) % CY, axis=1)
        before = pltpu.roll(hy[1], (2 * CY - MY - MY * k) % CY, axis=1)
        ext[k, :, CY:] = jnp.where(
            lane32 < MY, after, jnp.where(lane32 >= CY - MY, before, 0.0)
        )

    def around(ref, k):
        mid = ref[k]
        total = (
            pltpu.roll(mid, 1, axis=0)
            + pltpu.roll(mid, 31, axis=0)
            + pltpu.roll(mid, 1, axis=1)
            + pltpu.roll(mid, 2 * CY - 1, axis=1)
        )
        if k > 0:
            total = total + ref[k - 1]
        if k < NZ - 1:
            total = total + ref[k + 1]
        return mid, total

    odd = (
        lax.broadcasted_iota(jnp.int32, (32, 2 * CY), 0)
        + lax.broadcasted_iota(jnp.int32, (32, 2 * CY), 1)
    ) & 1
    for k in range(NZ):
        mid, near = around(ext, k)
        value = COUPLING * (mid + SMOOTHING * (near - 6.0 * mid) - BACKGROUND)
        src[k] = value
        u[k] = jnp.where(odd == (k & 1), value * (-1.0 / (6.0 + SCREENING)), 0.0)

    def half(colour):
        for k in range(NZ):
            mid, near = around(u, k)
            square = mid * mid
            r = near - (6.0 + SCREENING) * mid - CUBIC_TERM * square * mid - src[k]
            s = -(6.0 + SCREENING) - (3.0 * CUBIC_TERM) * square
            u[k] = jnp.where(odd == ((k + colour) & 1), mid - r / s, mid)

    half(1)

    def sweep(n, carry):
        half(0)
        half(1)
        return carry

    lax.fori_loop(0, SWEEPS - 1, sweep, 0)
    for k in range(NZ):
        field[k] = u[k, 8:24, 0:CY]
    for copy in first + second:
        copy.wait_send()


def shards(sizes, payload, cells, counts):
    f32 = jnp.float32
    vmem = pl.BlockSpec(memory_space=pltpu.VMEM)
    smem = pl.BlockSpec(memory_space=pltpu.SMEM)
    main, xs, ys, cs = pl.pallas_call(
        deposit_kernel,
        out_shape=(
            jax.ShapeDtypeStruct((4, NZ, CX, CY), f32),
            jax.ShapeDtypeStruct((2, 4, NZ * MX, CY), f32),
            jax.ShapeDtypeStruct((2, 4, CX, CY), f32),
            jax.ShapeDtypeStruct((4, 8, CY), f32),
        ),
        in_specs=[smem, vmem, vmem],
        out_specs=(vmem,) * 4,
        scratch_shapes=[
            pltpu.VMEM((8 * STAY, 2 * CY), f32),
            pltpu.VMEM((8 * LEAVE, 2 * CY), f32),
        ],
        compiler_params=pltpu.CompilerParams(vmem_limit_bytes=40 * 1024 * 1024),
        name="deposit",
    )(counts, payload, cells)
    field, momentum = pl.pallas_call(
        functools.partial(relax_kernel, sizes),
        out_shape=(
            jax.ShapeDtypeStruct((NZ, CX, CY), f32),
            jax.ShapeDtypeStruct((3, NZ, CX, CY), f32),
        ),
        in_specs=[vmem] * 4,
        out_specs=(vmem,) * 2,
        scratch_shapes=[
            pltpu.VMEM((2, 4, NZ * MX, CY), f32),
            pltpu.VMEM((2, 4, CX, CY), f32),
            pltpu.VMEM((4, 8, CY), f32),
            pltpu.VMEM((NZ, CX, CY), f32),
            pltpu.VMEM((2, CX, CY), f32),
            pltpu.VMEM((2, NZ, 8, CY), f32),
            pltpu.VMEM((2, 32, CY), f32),
            pltpu.VMEM((NZ, 32, 2 * CY), f32),
            pltpu.VMEM((NZ, 32, 2 * CY), f32),
            pltpu.VMEM((NZ, 32, 2 * CY), f32),
        ] + [pltpu.SemaphoreType.DMA((8,))] * 4,
        compiler_params=pltpu.CompilerParams(
            collective_id=0, has_side_effects=True, vmem_limit_bytes=40 * 1024 * 1024
        ),
        name="relax",
    )(main, xs, ys, cs)
    return field, momentum


def solution(mesh):
    sizes = (mesh.shape["gx"], mesh.shape["gy"])
    placed = (P(None, ("gx", "gy")), P(None, ("gx", "gy")), P(("gx", "gy"), None))
    return jax.shard_map(
        functools.partial(shards, sizes),
        mesh=mesh,
        in_specs=placed,
        out_specs=(P(None, "gx", "gy"), P(None, None, "gx", "gy")),
        check_vma=False,
    )
```

```python
import functools

import jax
import jax.numpy as jnp
from jax import lax
from jax.experimental import pallas as pl
from jax.experimental.pallas import tpu as pltpu
from jax.sharding import PartitionSpec as P

CX = 16
CY = 128
NZ = 8
SWEEPS = 4
MX = 2
MY = 16
HALO = 8
BLOCK = 1024
STAY = 64
LEAVE = 48

SCREENING = 0.5
CUBIC_TERM = 0.3
COUPLING = 1.5
SMOOTHING = 0.1
BACKGROUND = 1.0

MESH = pl.DeviceIdType.MESH
STEPS = ((1, 0), (-1, 0), (0, 1), (0, -1), (1, 1), (1, -1), (-1, 1), (-1, -1))


def deposit_kernel(
    counts, payload, cells, main, xs, ys, cs, stay_acc, leave_acc
):
    part = payload.shape[1]
    stay_acc[...] = jnp.zeros_like(stay_acc)
    leave_acc[...] = jnp.zeros_like(leave_acc)
    bf16 = jnp.bfloat16
    base = lax.broadcasted_iota(jnp.int32, (16, 128), 0)
    ids = [(base + 16 * g).astype(jnp.float32).astype(bf16) for g in range(16)]
    ids = [jnp.concatenate([v] * (BLOCK // 128), axis=1) for v in ids]
    one = jnp.ones((16, BLOCK), bf16)
    none = jnp.zeros((16, BLOCK), bf16)
    limits = []
    total = jnp.int32(0)
    for e in range(8):
        total = total + counts[0, e]
        limits.append(total)

    def packed(row):
        return jnp.broadcast_to(row.astype(jnp.float32), (16, BLOCK)).astype(bf16)

    def add(acc, count, span, row, col):
        col = packed(col)
        cols_hot = jnp.concatenate([jnp.where(v == col, one, none) for v in ids], axis=0)
        block = payload[:, span]
        first = lax.broadcasted_iota(jnp.int32, (4, BLOCK), 0) == 0
        values = block[0:1] * jnp.where(first, 1.0, block)
        high = values.astype(bf16).astype(jnp.float32)
        low = values - high
        wide = [packed(v[c : c + 1]) for v in (high, low) for c in range(4)]
        row = packed(row)
        masks = [ids[g] == row for g in range(count // 16)]
        left = jnp.concatenate([jnp.where(m, w, none) for w in wide for m in masks], axis=0)
        acc[...] += lax.dot_general(
            left, cols_hot, (((1,), (1,)), ((), ())), preferred_element_type=jnp.float32
        )

    def block_of(b):
        start = pl.multiple_of(b * BLOCK, BLOCK)
        span = pl.ds(start, BLOCK)
        position = start + lax.broadcasted_iota(jnp.int32, (1, BLOCK), 1)
        return span, position, cells[0:1, span], cells[1:2, span], cells[2:3, span]

    def stay_step(b, carry):
        span, position, k, i, j = block_of(b)
        row = jnp.where(position >= limits[7], k * 8 + (i & 7), 255)
        add(stay_acc, STAY, span, row, (i >> 3) * CY + j)
        return carry

    def leave_step(b, carry):
        span, position, k, i, j = block_of(b)
        direction = jnp.zeros((1, BLOCK), jnp.int32)
        for e in range(8):
            direction = direction + (position >= limits[e]).astype(jnp.int32)
        chunk = k * MY + (j & (MY - 1))
        layer = i & 1
        row = jnp.where(
            direction < 2, k * MX + layer, jnp.where(direction < 4, 16 + i, 28 + direction)
        )
        col = jnp.where(
            direction < 2,
            direction * CY + j,
            jnp.where(direction < 4, (direction - 2) * CY, layer * CY) + chunk,
        )
        row = jnp.where(direction == 8, 255, row)
        add(leave_acc, LEAVE, span, row, col)
        return carry

    blocks = part // BLOCK
    left_blocks = (limits[7] + (BLOCK - 1)) // BLOCK
    lax.fori_loop(0, left_blocks, leave_step, 0)
    lax.fori_loop(limits[7] // BLOCK, blocks, stay_step, 0)
    for c in range(4):
        for h in range(2):
            lanes = slice(h * CY, (h + 1) * CY)
            whole = (
                stay_acc[c * STAY : (c + 1) * STAY, lanes]
                + stay_acc[(4 + c) * STAY : (5 + c) * STAY, lanes]
            )
            main[c, :, 8 * h : 8 * h + 8, :] = whole.reshape(NZ, 8, CY)
            out = (
                leave_acc[c * LEAVE : (c + 1) * LEAVE, lanes]
                + leave_acc[(4 + c) * LEAVE : (5 + c) * LEAVE, lanes]
            )
            xs[h, c] = out[0:16]
            ys[h, c] = out[16:32]
            for d in range(4):
                cs[d, 2 * c + h : 2 * c + h + 1, :] = out[32 + d : 33 + d]


def relax_kernel(
    sizes, main, xs, ys, cs, field, momentum,
    rx, ry, rc, dens, edges, hx, hy, ext, src, u,
    send1, recv1, send2, recv2,
):
    n_gx, n_gy = sizes
    me_x = lax.axis_index("gx")
    me_y = lax.axis_index("gy")

    def device(step):
        return (lax.rem(me_x + step[0] + n_gx, n_gx), lax.rem(me_y + step[1] + n_gy, n_gy))

    barrier = pltpu.get_barrier_semaphore()
    for step in STEPS:
        pl.semaphore_signal(barrier, inc=1, device_id=device(step), device_id_type=MESH)
    pl.semaphore_wait(barrier, 8)

    def remote(src_ref, dst_ref, sems, recvs, d):
        return pltpu.make_async_remote_copy(
            src_ref=src_ref, dst_ref=dst_ref, send_sem=sems.at[d], recv_sem=recvs.at[d],
            device_id=device(STEPS[d]), device_id_type=MESH,
        )

    first = []
    for d in range(8):
        if d < 2:
            pair = (xs.at[d], rx.at[d])
        elif d < 4:
            pair = (ys.at[d - 2], ry.at[d - 2])
        else:
            pair = (cs.at[d - 4], rc.at[d - 4])
        first.append(remote(pair[0], pair[1], send1, recv1, d))
    for copy in first:
        copy.start()
    lane = lax.broadcasted_iota(jnp.int32, (1, CY), 1)
    lane16 = lax.broadcasted_iota(jnp.int32, (CX, CY), 1)
    for copy in first:
        copy.wait_recv()

    def collected(c):
        sides = []
        for s in range(2):
            low = rc[s, 2 * c : 2 * c + 2, :]
            high = rc[2 + s, 2 * c : 2 * c + 2, :]
            pad = jnp.zeros((CX - 2 * MX, CY), jnp.float32)
            sides.append(ry[s, c] + jnp.concatenate([low, pad, high], axis=0))
        pad = jnp.zeros((CX - 2 * MX, CY), jnp.float32)
        out = []
        for k in range(NZ):
            left = pltpu.roll(sides[0], (CY - MY * k) % CY, axis=1)
            right = pltpu.roll(sides[1], (2 * CY - MY - MY * k) % CY, axis=1)
            extra = jnp.where(lane16 < MY, left, jnp.where(lane16 >= CY - MY, right, 0.0))
            faces = jnp.concatenate(
                [rx[0, c, 2 * k : 2 * k + 2, :], pad, rx[1, c, 2 * k : 2 * k + 2, :]], axis=0
            )
            out.append(main[c, k] + faces + extra)
        return out

    rho = collected(0)
    low_edge = jnp.zeros((CX, CY), jnp.float32)
    high_edge = jnp.zeros((CX, CY), jnp.float32)
    for k in range(NZ):
        dens[k] = rho[k]
        here = (lane16 >= MY * k) & (lane16 < MY * (k + 1))
        low_edge = jnp.where(here, pltpu.roll(rho[k], MY * k, axis=1), low_edge)
        high_edge = jnp.where(here, pltpu.roll(rho[k], (MY * (k + 1)) % CY, axis=1), high_edge)
    edges[0] = low_edge
    edges[1] = high_edge

    second = [
        (dens.at[:, 8:16, :], hx.at[0]),
        (dens.at[:, 0:8, :], hx.at[1]),
        (edges.at[1], hy.at[1, 8:24, :]),
        (edges.at[0], hy.at[0, 8:24, :]),
        (edges.at[1, 8:16, :], hy.at[1, 0:8, :]),
        (edges.at[0, 8:16, :], hy.at[0, 0:8, :]),
        (edges.at[1, 0:8, :], hy.at[1, 24:32, :]),
        (edges.at[0, 0:8, :], hy.at[0, 24:32, :]),
    ]
    second = [remote(a, b, send2, recv2, d) for d, (a, b) in enumerate(second)]
    for copy in second:
        copy.start()
    for c in range(1, 4):
        for k, layer in enumerate(collected(c)):
            momentum[c - 1, k] = layer
    for copy in second:
        copy.wait_recv()

    lane32 = lax.broadcasted_iota(jnp.int32, (32, CY), 1)
    for k in range(NZ):
        ext[k, 0:8, 0:CY] = hx[0, k]
        ext[k, 8:24, 0:CY] = dens[k]
        ext[k, 24:32, 0:CY] = hx[1, k]
        after = pltpu.roll(hy[0], (CY - MY * k) % CY, axis=1)
        before = pltpu.roll(hy[1], (2 * CY - MY - MY * k) % CY, axis=1)
        ext[k, :, CY:] = jnp.where(
            lane32 < MY, after, jnp.where(lane32 >= CY - MY, before, 0.0)
        )

    def around(ref, k):
        mid = ref[k]
        total = (
            pltpu.roll(mid, 1, axis=0)
            + pltpu.roll(mid, 31, axis=0)
            + pltpu.roll(mid, 1, axis=1)
            + pltpu.roll(mid, 2 * CY - 1, axis=1)
        )
        if k > 0:
            total = total + ref[k - 1]
        if k < NZ - 1:
            total = total + ref[k + 1]
        return mid, total

    odd = (
        lax.broadcasted_iota(jnp.int32, (32, 2 * CY), 0)
        + lax.broadcasted_iota(jnp.int32, (32, 2 * CY), 1)
    ) & 1
    for k in range(NZ):
        mid, near = around(ext, k)
        value = COUPLING * (mid + SMOOTHING * (near - 6.0 * mid) - BACKGROUND)
        src[k] = value
        u[k] = jnp.where(odd == (k & 1), value * (-1.0 / (6.0 + SCREENING)), 0.0)

    def relaxed(mid, near, source):
        square = mid * mid
        slope = (6.0 + SCREENING) + (3.0 * CUBIC_TERM) * square
        r = near - source - mid * ((6.0 + SCREENING) + CUBIC_TERM * square)
        inverse = pl.reciprocal(slope, approx=True)
        inverse = inverse * (2.0 - slope * inverse)
        return mid + r * inverse

    def half(colour):
        for k in range(NZ):
            mid, near = around(u, k)
            new = relaxed(mid, near, src[k])
            u[k] = jnp.where(odd == ((k + colour) & 1), new, mid)

    def sweep(n, carry):
        half(1)
        half(0)
        return carry

    lax.fori_loop(0, SWEEPS - 1, sweep, 0)
    odd_tile = odd[8:24, 0:CY]
    for k in range(NZ):
        wide = u[k, 8:24, :]
        mid = wide[:, 0:CY]
        near = (
            u[k, 7:23, 0:CY]
            + u[k, 9:25, 0:CY]
            + pltpu.roll(wide, 1, axis=1)[:, 0:CY]
            + pltpu.roll(wide, 2 * CY - 1, axis=1)[:, 0:CY]
        )
        if k > 0:
            near = near + u[k - 1, 8:24, 0:CY]
        if k < NZ - 1:
            near = near + u[k + 1, 8:24, 0:CY]
        new = relaxed(mid, near, src[k, 8:24, 0:CY])
        field[k] = jnp.where(odd_tile == ((k + 1) & 1), new, mid)
    for copy in first + second:
        copy.wait_send()


def shards(sizes, payload, cells, counts):
    f32 = jnp.float32
    vmem = pl.BlockSpec(memory_space=pltpu.VMEM)
    main, xs, ys, cs = pl.pallas_call(
        deposit_kernel,
        out_shape=(
            jax.ShapeDtypeStruct((4, NZ, CX, CY), f32),
            jax.ShapeDtypeStruct((2, 4, NZ * MX, CY), f32),
            jax.ShapeDtypeStruct((2, 4, CX, CY), f32),
            jax.ShapeDtypeStruct((4, 8, CY), f32),
        ),
        in_specs=[pl.BlockSpec(memory_space=pltpu.SMEM), vmem, vmem],
        out_specs=(vmem,) * 4,
        scratch_shapes=[
            pltpu.VMEM((8 * STAY, 2 * CY), f32),
            pltpu.VMEM((8 * LEAVE, 2 * CY), f32),
        ],
        compiler_params=pltpu.CompilerParams(vmem_limit_bytes=40 * 1024 * 1024),
        name="deposit",
    )(counts, payload, cells)
    field, momentum = pl.pallas_call(
        functools.partial(relax_kernel, sizes),
        out_shape=(
            jax.ShapeDtypeStruct((NZ, CX, CY), f32),
            jax.ShapeDtypeStruct((3, NZ, CX, CY), f32),
        ),
        in_specs=[vmem] * 4,
        out_specs=(vmem,) * 2,
        scratch_shapes=[
            pltpu.VMEM((2, 4, NZ * MX, CY), f32),
            pltpu.VMEM((2, 4, CX, CY), f32),
            pltpu.VMEM((4, 8, CY), f32),
            pltpu.VMEM((NZ, CX, CY), f32),
            pltpu.VMEM((2, CX, CY), f32),
            pltpu.VMEM((2, NZ, 8, CY), f32),
            pltpu.VMEM((2, 32, CY), f32),
            pltpu.VMEM((NZ, 32, 2 * CY), f32),
            pltpu.VMEM((NZ, 32, 2 * CY), f32),
            pltpu.VMEM((NZ, 32, 2 * CY), f32),
        ] + [pltpu.SemaphoreType.DMA((8,))] * 4,
        compiler_params=pltpu.CompilerParams(
            collective_id=0, has_side_effects=True, vmem_limit_bytes=40 * 1024 * 1024
        ),
        name="relax",
    )(main, xs, ys, cs)
    return field, momentum


def solution(mesh):
    sizes = (mesh.shape["gx"], mesh.shape["gy"])
    placed = (P(None, ("gx", "gy")), P(None, ("gx", "gy")), P(("gx", "gy"), None))
    return jax.shard_map(
        functools.partial(shards, sizes),
        mesh=mesh,
        in_specs=placed,
        out_specs=(P(None, "gx", "gy"), P(None, None, "gx", "gy")),
        check_vma=False,
    )
```

```python
import functools

import jax
import jax.numpy as jnp
from jax import lax
from jax.experimental import pallas as pl
from jax.experimental.pallas import tpu as pltpu
from jax.sharding import PartitionSpec as P

CX = 16
CY = 128
NZ = 8
SWEEPS = 4
MX = 2
MY = 16
HALO = 8
BLOCK = 1024
STAY = 64
LEAVE = 48

SCREENING = 0.5
CUBIC_TERM = 0.3
COUPLING = 1.5
SMOOTHING = 0.1
BACKGROUND = 1.0

MESH = pl.DeviceIdType.MESH
STEPS = ((1, 0), (-1, 0), (0, 1), (0, -1), (1, 1), (1, -1), (-1, 1), (-1, -1))


def deposit_kernel(
    counts_hbm, payload_hbm, cells_hbm, main, xs, ys, cs,
    stay_acc, leave_acc, counts, payload, cells, sems,
):
    part = payload.shape[1]
    copies = [
        pltpu.make_async_copy(counts_hbm, counts, sems.at[0]),
        pltpu.make_async_copy(cells_hbm, cells, sems.at[1]),
        pltpu.make_async_copy(payload_hbm, payload, sems.at[2]),
    ]
    for copy in copies:
        copy.start()
    stay_acc[...] = jnp.zeros_like(stay_acc)
    leave_acc[...] = jnp.zeros_like(leave_acc)
    bf16 = jnp.bfloat16
    base = lax.broadcasted_iota(jnp.int32, (16, 128), 0)
    ids = [(base + 16 * g).astype(jnp.float32).astype(bf16) for g in range(16)]
    ids = [jnp.concatenate([v] * (BLOCK // 128), axis=1) for v in ids]
    one = jnp.ones((16, BLOCK), bf16)
    none = jnp.zeros((16, BLOCK), bf16)
    for copy in copies:
        copy.wait()
    limits = []
    total = jnp.int32(0)
    for e in range(8):
        total = total + counts[0, e]
        limits.append(total)

    def packed(row):
        return jnp.broadcast_to(row.astype(jnp.float32), (16, BLOCK)).astype(bf16)

    def add(acc, count, span, row, col):
        col = packed(col)
        cols_hot = jnp.concatenate([jnp.where(v == col, one, none) for v in ids], axis=0)
        block = payload[:, span]
        first = lax.broadcasted_iota(jnp.int32, (4, BLOCK), 0) == 0
        values = block[0:1] * jnp.where(first, 1.0, block)
        high = values.astype(bf16).astype(jnp.float32)
        low = values - high
        wide = [packed(v[c : c + 1]) for v in (high, low) for c in range(4)]
        row = packed(row)
        masks = [ids[g] == row for g in range(count // 16)]
        left = jnp.concatenate([jnp.where(m, w, none) for w in wide for m in masks], axis=0)
        acc[...] += lax.dot_general(
            left, cols_hot, (((1,), (1,)), ((), ())), preferred_element_type=jnp.float32
        )

    def block_of(b):
        start = pl.multiple_of(b * BLOCK, BLOCK)
        span = pl.ds(start, BLOCK)
        position = start + lax.broadcasted_iota(jnp.int32, (1, BLOCK), 1)
        return span, position, cells[0:1, span], cells[1:2, span], cells[2:3, span]

    def stay_step(b, carry):
        span, position, k, i, j = block_of(b)
        row = jnp.where(position >= limits[7], k * 8 + (i & 7), 255)
        add(stay_acc, STAY, span, row, (i >> 3) * CY + j)
        return carry

    def leave_step(b, carry):
        span, position, k, i, j = block_of(b)
        direction = jnp.zeros((1, BLOCK), jnp.int32)
        for e in range(8):
            direction = direction + (position >= limits[e]).astype(jnp.int32)
        chunk = k * MY + (j & (MY - 1))
        layer = i & 1
        row = jnp.where(
            direction < 2, k * MX + layer, jnp.where(direction < 4, 16 + i, 28 + direction)
        )
        col = jnp.where(
            direction < 2,
            direction * CY + j,
            jnp.where(direction < 4, (direction - 2) * CY, layer * CY) + chunk,
        )
        row = jnp.where(direction == 8, 255, row)
        add(leave_acc, LEAVE, span, row, col)
        return carry

    blocks = part // BLOCK
    left_blocks = (limits[7] + (BLOCK - 1)) // BLOCK
    lax.fori_loop(0, left_blocks, leave_step, 0)
    lax.fori_loop(limits[7] // BLOCK, blocks, stay_step, 0)
    for c in range(4):
        for h in range(2):
            lanes = slice(h * CY, (h + 1) * CY)
            whole = (
                stay_acc[c * STAY : (c + 1) * STAY, lanes]
                + stay_acc[(4 + c) * STAY : (5 + c) * STAY, lanes]
            )
            main[c, :, 8 * h : 8 * h + 8, :] = whole.reshape(NZ, 8, CY)
            out = (
                leave_acc[c * LEAVE : (c + 1) * LEAVE, lanes]
                + leave_acc[(4 + c) * LEAVE : (5 + c) * LEAVE, lanes]
            )
            xs[h, c] = out[0:16]
            ys[h, c] = out[16:32]
            for d in range(4):
                cs[d, 2 * c + h : 2 * c + h + 1, :] = out[32 + d : 33 + d]


def relax_kernel(
    sizes, main, xs, ys, cs, field, momentum,
    rx, ry, rc, dens, edges, hx, hy, ext, src, u,
    send1, recv1, send2, recv2,
):
    n_gx, n_gy = sizes
    me_x = lax.axis_index("gx")
    me_y = lax.axis_index("gy")

    def device(step):
        return (lax.rem(me_x + step[0] + n_gx, n_gx), lax.rem(me_y + step[1] + n_gy, n_gy))

    barrier = pltpu.get_barrier_semaphore()
    for step in STEPS:
        pl.semaphore_signal(barrier, inc=1, device_id=device(step), device_id_type=MESH)
    pl.semaphore_wait(barrier, 8)

    def remote(src_ref, dst_ref, sems, recvs, d):
        return pltpu.make_async_remote_copy(
            src_ref=src_ref, dst_ref=dst_ref, send_sem=sems.at[d], recv_sem=recvs.at[d],
            device_id=device(STEPS[d]), device_id_type=MESH,
        )

    first = []
    for d in range(8):
        if d < 2:
            pair = (xs.at[d], rx.at[d])
        elif d < 4:
            pair = (ys.at[d - 2], ry.at[d - 2])
        else:
            pair = (cs.at[d - 4], rc.at[d - 4])
        first.append(remote(pair[0], pair[1], send1, recv1, d))
    for copy in first:
        copy.start()
    lane = lax.broadcasted_iota(jnp.int32, (1, CY), 1)
    lane16 = lax.broadcasted_iota(jnp.int32, (CX, CY), 1)
    for copy in first:
        copy.wait_recv()

    def collected(c):
        sides = []
        for s in range(2):
            low = rc[s, 2 * c : 2 * c + 2, :]
            high = rc[2 + s, 2 * c : 2 * c + 2, :]
            pad = jnp.zeros((CX - 2 * MX, CY), jnp.float32)
            sides.append(ry[s, c] + jnp.concatenate([low, pad, high], axis=0))
        pad = jnp.zeros((CX - 2 * MX, CY), jnp.float32)
        out = []
        for k in range(NZ):
            left = pltpu.roll(sides[0], (CY - MY * k) % CY, axis=1)
            right = pltpu.roll(sides[1], (2 * CY - MY - MY * k) % CY, axis=1)
            extra = jnp.where(lane16 < MY, left, jnp.where(lane16 >= CY - MY, right, 0.0))
            faces = jnp.concatenate(
                [rx[0, c, 2 * k : 2 * k + 2, :], pad, rx[1, c, 2 * k : 2 * k + 2, :]], axis=0
            )
            out.append(main[c, k] + faces + extra)
        return out

    rho = collected(0)
    low_edge = jnp.zeros((CX, CY), jnp.float32)
    high_edge = jnp.zeros((CX, CY), jnp.float32)
    for k in range(NZ):
        dens[k] = rho[k]
        here = (lane16 >= MY * k) & (lane16 < MY * (k + 1))
        low_edge = jnp.where(here, pltpu.roll(rho[k], MY * k, axis=1), low_edge)
        high_edge = jnp.where(here, pltpu.roll(rho[k], (MY * (k + 1)) % CY, axis=1), high_edge)
    edges[0] = low_edge
    edges[1] = high_edge

    second = [
        (dens.at[:, 8:16, :], hx.at[0]),
        (dens.at[:, 0:8, :], hx.at[1]),
        (edges.at[1], hy.at[1, 8:24, :]),
        (edges.at[0], hy.at[0, 8:24, :]),
        (edges.at[1, 8:16, :], hy.at[1, 0:8, :]),
        (edges.at[0, 8:16, :], hy.at[0, 0:8, :]),
        (edges.at[1, 0:8, :], hy.at[1, 24:32, :]),
        (edges.at[0, 0:8, :], hy.at[0, 24:32, :]),
    ]
    second = [remote(a, b, send2, recv2, d) for d, (a, b) in enumerate(second)]
    for copy in second:
        copy.start()
    for c in range(1, 4):
        for k, layer in enumerate(collected(c)):
            momentum[c - 1, k] = layer
    for copy in second:
        copy.wait_recv()

    lane32 = lax.broadcasted_iota(jnp.int32, (32, CY), 1)
    for k in range(NZ):
        ext[k, 0:8, 0:CY] = hx[0, k]
        ext[k, 8:24, 0:CY] = dens[k]
        ext[k, 24:32, 0:CY] = hx[1, k]
        after = pltpu.roll(hy[0], (CY - MY * k) % CY, axis=1)
        before = pltpu.roll(hy[1], (2 * CY - MY - MY * k) % CY, axis=1)
        ext[k, :, CY:] = jnp.where(
            lane32 < MY, after, jnp.where(lane32 >= CY - MY, before, 0.0)
        )

    def around(ref, k):
        mid = ref[k]
        total = (
            pltpu.roll(mid, 1, axis=0)
            + pltpu.roll(mid, 31, axis=0)
            + pltpu.roll(mid, 1, axis=1)
            + pltpu.roll(mid, 2 * CY - 1, axis=1)
        )
        if k > 0:
            total = total + ref[k - 1]
        if k < NZ - 1:
            total = total + ref[k + 1]
        return mid, total

    odd = (
        lax.broadcasted_iota(jnp.int32, (32, 2 * CY), 0)
        + lax.broadcasted_iota(jnp.int32, (32, 2 * CY), 1)
    ) & 1
    for k in range(NZ):
        mid, near = around(ext, k)
        value = COUPLING * (mid + SMOOTHING * (near - 6.0 * mid) - BACKGROUND)
        src[k] = value
        u[k] = jnp.where(odd == (k & 1), value * (-1.0 / (6.0 + SCREENING)), 0.0)

    def relaxed(mid, near, source):
        square = mid * mid
        slope = (6.0 + SCREENING) + (3.0 * CUBIC_TERM) * square
        r = near - source - mid * ((6.0 + SCREENING) + CUBIC_TERM * square)
        inverse = pl.reciprocal(slope, approx=True)
        inverse = inverse * (2.0 - slope * inverse)
        return mid + r * inverse

    def half(colour):
        for k in range(NZ):
            mid, near = around(u, k)
            new = relaxed(mid, near, src[k])
            u[k] = jnp.where(odd == ((k + colour) & 1), new, mid)

    def sweep(n, carry):
        half(1)
        half(0)
        return carry

    lax.fori_loop(0, SWEEPS - 1, sweep, 0)
    odd_tile = odd[8:24, 0:CY]
    for k in range(NZ):
        wide = u[k, 8:24, :]
        mid = wide[:, 0:CY]
        near = (
            u[k, 7:23, 0:CY]
            + u[k, 9:25, 0:CY]
            + pltpu.roll(wide, 1, axis=1)[:, 0:CY]
            + pltpu.roll(wide, 2 * CY - 1, axis=1)[:, 0:CY]
        )
        if k > 0:
            near = near + u[k - 1, 8:24, 0:CY]
        if k < NZ - 1:
            near = near + u[k + 1, 8:24, 0:CY]
        new = relaxed(mid, near, src[k, 8:24, 0:CY])
        field[k] = jnp.where(odd_tile == ((k + 1) & 1), new, mid)
    for copy in first + second:
        copy.wait_send()


def shards(sizes, payload, cells, counts):
    f32 = jnp.float32
    vmem = pl.BlockSpec(memory_space=pltpu.VMEM)
    main, xs, ys, cs = pl.pallas_call(
        deposit_kernel,
        out_shape=(
            jax.ShapeDtypeStruct((4, NZ, CX, CY), f32),
            jax.ShapeDtypeStruct((2, 4, NZ * MX, CY), f32),
            jax.ShapeDtypeStruct((2, 4, CX, CY), f32),
            jax.ShapeDtypeStruct((4, 8, CY), f32),
        ),
        in_specs=[pl.BlockSpec(memory_space=pltpu.HBM)] * 3,
        out_specs=(vmem,) * 4,
        scratch_shapes=[
            pltpu.VMEM((8 * STAY, 2 * CY), f32),
            pltpu.VMEM((8 * LEAVE, 2 * CY), f32),
            pltpu.SMEM(counts.shape, jnp.int32),
            pltpu.VMEM(payload.shape, f32),
            pltpu.VMEM(cells.shape, jnp.int32),
            pltpu.SemaphoreType.DMA((3,)),
        ],
        compiler_params=pltpu.CompilerParams(vmem_limit_bytes=40 * 1024 * 1024),
        name="deposit",
    )(*[pltpu.with_memory_space_constraint(a, pltpu.HBM) for a in (counts, payload, cells)])
    field, momentum = pl.pallas_call(
        functools.partial(relax_kernel, sizes),
        out_shape=(
            jax.ShapeDtypeStruct((NZ, CX, CY), f32),
            jax.ShapeDtypeStruct((3, NZ, CX, CY), f32),
        ),
        in_specs=[vmem] * 4,
        out_specs=(vmem,) * 2,
        scratch_shapes=[
            pltpu.VMEM((2, 4, NZ * MX, CY), f32),
            pltpu.VMEM((2, 4, CX, CY), f32),
            pltpu.VMEM((4, 8, CY), f32),
            pltpu.VMEM((NZ, CX, CY), f32),
            pltpu.VMEM((2, CX, CY), f32),
            pltpu.VMEM((2, NZ, 8, CY), f32),
            pltpu.VMEM((2, 32, CY), f32),
            pltpu.VMEM((NZ, 32, 2 * CY), f32),
            pltpu.VMEM((NZ, 32, 2 * CY), f32),
            pltpu.VMEM((NZ, 32, 2 * CY), f32),
        ] + [pltpu.SemaphoreType.DMA((8,))] * 4,
        compiler_params=pltpu.CompilerParams(
            collective_id=0, has_side_effects=True, vmem_limit_bytes=40 * 1024 * 1024
        ),
        name="relax",
    )(main, xs, ys, cs)
    return field, momentum


def solution(mesh):
    sizes = (mesh.shape["gx"], mesh.shape["gy"])
    placed = (P(None, ("gx", "gy")), P(None, ("gx", "gy")), P(("gx", "gy"), None))
    return jax.shard_map(
        functools.partial(shards, sizes),
        mesh=mesh,
        in_specs=placed,
        out_specs=(P(None, "gx", "gy"), P(None, None, "gx", "gy")),
        check_vma=False,
    )
```

```python
import functools

import jax
import jax.numpy as jnp
from jax import lax
from jax.experimental import pallas as pl
from jax.experimental.pallas import tpu as pltpu
from jax.sharding import PartitionSpec as P

CX = 16
CY = 128
NZ = 8
SWEEPS = 4
MX = 2
MY = 16
HALO = 8
BLOCK = 2048
STAY = 64
LEAVE = 48

SCREENING = 0.5
CUBIC_TERM = 0.3
COUPLING = 1.5
SMOOTHING = 0.1
BACKGROUND = 1.0

MESH = pl.DeviceIdType.MESH
STEPS = ((1, 0), (-1, 0), (0, 1), (0, -1), (1, 1), (1, -1), (-1, 1), (-1, -1))


def deposit_kernel(
    counts_hbm, payload_hbm, cells_hbm, main, xs, ys, cs,
    stay_acc, leave_acc, counts, payload, cells, sems,
):
    part = payload.shape[1]
    copies = [
        pltpu.make_async_copy(counts_hbm, counts, sems.at[0]),
        pltpu.make_async_copy(cells_hbm, cells, sems.at[1]),
        pltpu.make_async_copy(payload_hbm, payload, sems.at[2]),
    ]
    for copy in copies:
        copy.start()
    stay_acc[...] = jnp.zeros_like(stay_acc)
    leave_acc[...] = jnp.zeros_like(leave_acc)
    bf16 = jnp.bfloat16
    base = lax.broadcasted_iota(jnp.int32, (16, 128), 0)
    ids = [(base + 16 * g).astype(jnp.float32).astype(bf16) for g in range(16)]
    ids = [jnp.concatenate([v] * (BLOCK // 128), axis=1) for v in ids]
    one = jnp.ones((16, BLOCK), bf16)
    none = jnp.zeros((16, BLOCK), bf16)
    for copy in copies:
        copy.wait()
    limits = []
    total = jnp.int32(0)
    for e in range(8):
        total = total + counts[0, e]
        limits.append(total)

    def packed(row):
        return jnp.broadcast_to(row.astype(jnp.float32), (16, BLOCK)).astype(bf16)

    def add(acc, count, span, row, col):
        col = packed(col)
        cols_hot = jnp.concatenate([jnp.where(v == col, one, none) for v in ids], axis=0)
        block = payload[:, span]
        first = lax.broadcasted_iota(jnp.int32, (4, BLOCK), 0) == 0
        values = block[0:1] * jnp.where(first, 1.0, block)
        high = values.astype(bf16).astype(jnp.float32)
        low = values - high
        wide = [packed(v[c : c + 1]) for v in (high, low) for c in range(4)]
        row = packed(row)
        masks = [ids[g] == row for g in range(count // 16)]
        left = jnp.concatenate([jnp.where(m, w, none) for w in wide for m in masks], axis=0)
        acc[...] += lax.dot_general(
            left, cols_hot, (((1,), (1,)), ((), ())), preferred_element_type=jnp.float32
        )

    def block_of(b):
        start = pl.multiple_of(b * BLOCK, BLOCK)
        span = pl.ds(start, BLOCK)
        position = start + lax.broadcasted_iota(jnp.int32, (1, BLOCK), 1)
        return span, position, cells[0:1, span], cells[1:2, span], cells[2:3, span]

    def stay_step(b, carry):
        span, position, k, i, j = block_of(b)
        row = jnp.where(position >= limits[7], k * 8 + (i & 7), 255)
        add(stay_acc, STAY, span, row, (i >> 3) * CY + j)
        return carry

    def leave_step(b, carry):
        span, position, k, i, j = block_of(b)
        direction = jnp.zeros((1, BLOCK), jnp.int32)
        for e in range(8):
            direction = direction + (position >= limits[e]).astype(jnp.int32)
        chunk = k * MY + (j & (MY - 1))
        layer = i & 1
        row = jnp.where(
            direction < 2, k * MX + layer, jnp.where(direction < 4, 16 + i, 28 + direction)
        )
        col = jnp.where(
            direction < 2,
            direction * CY + j,
            jnp.where(direction < 4, (direction - 2) * CY, layer * CY) + chunk,
        )
        row = jnp.where(direction == 8, 255, row)
        add(leave_acc, LEAVE, span, row, col)
        return carry

    blocks = part // BLOCK
    left_blocks = (limits[7] + (BLOCK - 1)) // BLOCK
    lax.fori_loop(0, left_blocks, leave_step, 0)
    lax.fori_loop(limits[7] // BLOCK, blocks, stay_step, 0)
    for c in range(4):
        for h in range(2):
            lanes = slice(h * CY, (h + 1) * CY)
            whole = (
                stay_acc[c * STAY : (c + 1) * STAY, lanes]
                + stay_acc[(4 + c) * STAY : (5 + c) * STAY, lanes]
            )
            main[c, :, 8 * h : 8 * h + 8, :] = whole.reshape(NZ, 8, CY)
            out = (
                leave_acc[c * LEAVE : (c + 1) * LEAVE, lanes]
                + leave_acc[(4 + c) * LEAVE : (5 + c) * LEAVE, lanes]
            )
            xs[h, c] = out[0:16]
            ys[h, c] = out[16:32]
            for d in range(4):
                cs[d, 2 * c + h : 2 * c + h + 1, :] = out[32 + d : 33 + d]


def relax_kernel(
    sizes, main, xs, ys, cs, field, momentum,
    rx, ry, rc, dens, edges, hx, hy, ext, src, u,
    send1, recv1, send2, recv2,
):
    n_gx, n_gy = sizes
    me_x = lax.axis_index("gx")
    me_y = lax.axis_index("gy")

    def device(step):
        return (lax.rem(me_x + step[0] + n_gx, n_gx), lax.rem(me_y + step[1] + n_gy, n_gy))

    barrier = pltpu.get_barrier_semaphore()
    for step in STEPS:
        pl.semaphore_signal(barrier, inc=1, device_id=device(step), device_id_type=MESH)
    pl.semaphore_wait(barrier, 8)

    def remote(src_ref, dst_ref, sems, recvs, d):
        return pltpu.make_async_remote_copy(
            src_ref=src_ref, dst_ref=dst_ref, send_sem=sems.at[d], recv_sem=recvs.at[d],
            device_id=device(STEPS[d]), device_id_type=MESH,
        )

    first = []
    for d in range(8):
        if d < 2:
            pair = (xs.at[d], rx.at[d])
        elif d < 4:
            pair = (ys.at[d - 2], ry.at[d - 2])
        else:
            pair = (cs.at[d - 4], rc.at[d - 4])
        first.append(remote(pair[0], pair[1], send1, recv1, d))
    for copy in first:
        copy.start()
    lane = lax.broadcasted_iota(jnp.int32, (1, CY), 1)
    lane16 = lax.broadcasted_iota(jnp.int32, (CX, CY), 1)
    for copy in first:
        copy.wait_recv()

    def collected(c):
        sides = []
        for s in range(2):
            low = rc[s, 2 * c : 2 * c + 2, :]
            high = rc[2 + s, 2 * c : 2 * c + 2, :]
            pad = jnp.zeros((CX - 2 * MX, CY), jnp.float32)
            sides.append(ry[s, c] + jnp.concatenate([low, pad, high], axis=0))
        pad = jnp.zeros((CX - 2 * MX, CY), jnp.float32)
        out = []
        for k in range(NZ):
            left = pltpu.roll(sides[0], (CY - MY * k) % CY, axis=1)
            right = pltpu.roll(sides[1], (2 * CY - MY - MY * k) % CY, axis=1)
            extra = jnp.where(lane16 < MY, left, jnp.where(lane16 >= CY - MY, right, 0.0))
            faces = jnp.concatenate(
                [rx[0, c, 2 * k : 2 * k + 2, :], pad, rx[1, c, 2 * k : 2 * k + 2, :]], axis=0
            )
            out.append(main[c, k] + faces + extra)
        return out

    rho = collected(0)
    low_edge = jnp.zeros((CX, CY), jnp.float32)
    high_edge = jnp.zeros((CX, CY), jnp.float32)
    for k in range(NZ):
        dens[k] = rho[k]
        here = (lane16 >= MY * k) & (lane16 < MY * (k + 1))
        low_edge = jnp.where(here, pltpu.roll(rho[k], MY * k, axis=1), low_edge)
        high_edge = jnp.where(here, pltpu.roll(rho[k], (MY * (k + 1)) % CY, axis=1), high_edge)
    edges[0] = low_edge
    edges[1] = high_edge

    second = [
        (dens.at[:, 8:16, :], hx.at[0]),
        (dens.at[:, 0:8, :], hx.at[1]),
        (edges.at[1], hy.at[1, 8:24, :]),
        (edges.at[0], hy.at[0, 8:24, :]),
        (edges.at[1, 8:16, :], hy.at[1, 0:8, :]),
        (edges.at[0, 8:16, :], hy.at[0, 0:8, :]),
        (edges.at[1, 0:8, :], hy.at[1, 24:32, :]),
        (edges.at[0, 0:8, :], hy.at[0, 24:32, :]),
    ]
    second = [remote(a, b, send2, recv2, d) for d, (a, b) in enumerate(second)]
    for copy in second:
        copy.start()
    for c in range(1, 4):
        for k, layer in enumerate(collected(c)):
            momentum[c - 1, k] = layer
    for copy in second:
        copy.wait_recv()

    lane32 = lax.broadcasted_iota(jnp.int32, (32, CY), 1)
    for k in range(NZ):
        ext[k, 0:8, 0:CY] = hx[0, k]
        ext[k, 8:24, 0:CY] = dens[k]
        ext[k, 24:32, 0:CY] = hx[1, k]
        after = pltpu.roll(hy[0], (CY - MY * k) % CY, axis=1)
        before = pltpu.roll(hy[1], (2 * CY - MY - MY * k) % CY, axis=1)
        ext[k, :, CY:] = jnp.where(
            lane32 < MY, after, jnp.where(lane32 >= CY - MY, before, 0.0)
        )

    def around(ref, k):
        mid = ref[k]
        total = (
            pltpu.roll(mid, 1, axis=0)
            + pltpu.roll(mid, 31, axis=0)
            + pltpu.roll(mid, 1, axis=1)
            + pltpu.roll(mid, 2 * CY - 1, axis=1)
        )
        if k > 0:
            total = total + ref[k - 1]
        if k < NZ - 1:
            total = total + ref[k + 1]
        return mid, total

    odd = (
        lax.broadcasted_iota(jnp.int32, (32, 2 * CY), 0)
        + lax.broadcasted_iota(jnp.int32, (32, 2 * CY), 1)
    ) & 1
    for k in range(NZ):
        mid, near = around(ext, k)
        value = COUPLING * (mid + SMOOTHING * (near - 6.0 * mid) - BACKGROUND)
        src[k] = value
        u[k] = jnp.where(odd == (k & 1), value * (-1.0 / (6.0 + SCREENING)), 0.0)

    def relaxed(mid, near, source):
        square = mid * mid
        slope = (6.0 + SCREENING) + (3.0 * CUBIC_TERM) * square
        r = near - source - mid * ((6.0 + SCREENING) + CUBIC_TERM * square)
        inverse = pl.reciprocal(slope, approx=True)
        inverse = inverse * (2.0 - slope * inverse)
        return mid + r * inverse

    def half(colour):
        for k in range(NZ):
            mid, near = around(u, k)
            new = relaxed(mid, near, src[k])
            u[k] = jnp.where(odd == ((k + colour) & 1), new, mid)

    def sweep(n, carry):
        half(1)
        half(0)
        return carry

    lax.fori_loop(0, SWEEPS - 1, sweep, 0)
    odd_tile = odd[8:24, 0:CY]
    for k in range(NZ):
        wide = u[k, 8:24, :]
        mid = wide[:, 0:CY]
        near = (
            u[k, 7:23, 0:CY]
            + u[k, 9:25, 0:CY]
            + pltpu.roll(wide, 1, axis=1)[:, 0:CY]
            + pltpu.roll(wide, 2 * CY - 1, axis=1)[:, 0:CY]
        )
        if k > 0:
            near = near + u[k - 1, 8:24, 0:CY]
        if k < NZ - 1:
            near = near + u[k + 1, 8:24, 0:CY]
        new = relaxed(mid, near, src[k, 8:24, 0:CY])
        field[k] = jnp.where(odd_tile == ((k + 1) & 1), new, mid)
    for copy in first + second:
        copy.wait_send()


def shards(sizes, payload, cells, counts):
    f32 = jnp.float32
    vmem = pl.BlockSpec(memory_space=pltpu.VMEM)
    main, xs, ys, cs = pl.pallas_call(
        deposit_kernel,
        out_shape=(
            jax.ShapeDtypeStruct((4, NZ, CX, CY), f32),
            jax.ShapeDtypeStruct((2, 4, NZ * MX, CY), f32),
            jax.ShapeDtypeStruct((2, 4, CX, CY), f32),
            jax.ShapeDtypeStruct((4, 8, CY), f32),
        ),
        in_specs=[pl.BlockSpec(memory_space=pltpu.HBM)] * 3,
        out_specs=(vmem,) * 4,
        scratch_shapes=[
            pltpu.VMEM((8 * STAY, 2 * CY), f32),
            pltpu.VMEM((8 * LEAVE, 2 * CY), f32),
            pltpu.SMEM(counts.shape, jnp.int32),
            pltpu.VMEM(payload.shape, f32),
            pltpu.VMEM(cells.shape, jnp.int32),
            pltpu.SemaphoreType.DMA((3,)),
        ],
        compiler_params=pltpu.CompilerParams(vmem_limit_bytes=40 * 1024 * 1024),
        name="deposit",
    )(*[pltpu.with_memory_space_constraint(a, pltpu.HBM) for a in (counts, payload, cells)])
    field, momentum = pl.pallas_call(
        functools.partial(relax_kernel, sizes),
        out_shape=(
            jax.ShapeDtypeStruct((NZ, CX, CY), f32),
            jax.ShapeDtypeStruct((3, NZ, CX, CY), f32),
        ),
        in_specs=[vmem] * 4,
        out_specs=(vmem,) * 2,
        scratch_shapes=[
            pltpu.VMEM((2, 4, NZ * MX, CY), f32),
            pltpu.VMEM((2, 4, CX, CY), f32),
            pltpu.VMEM((4, 8, CY), f32),
            pltpu.VMEM((NZ, CX, CY), f32),
            pltpu.VMEM((2, CX, CY), f32),
            pltpu.VMEM((2, NZ, 8, CY), f32),
            pltpu.VMEM((2, 32, CY), f32),
            pltpu.VMEM((NZ, 32, 2 * CY), f32),
            pltpu.VMEM((NZ, 32, 2 * CY), f32),
            pltpu.VMEM((NZ, 32, 2 * CY), f32),
        ] + [pltpu.SemaphoreType.DMA((8,))] * 4,
        compiler_params=pltpu.CompilerParams(
            collective_id=0, has_side_effects=True, vmem_limit_bytes=40 * 1024 * 1024
        ),
        name="relax",
    )(main, xs, ys, cs)
    return field, momentum


def solution(mesh):
    sizes = (mesh.shape["gx"], mesh.shape["gy"])
    placed = (P(None, ("gx", "gy")), P(None, ("gx", "gy")), P(("gx", "gy"), None))
    return jax.shard_map(
        functools.partial(shards, sizes),
        mesh=mesh,
        in_specs=placed,
        out_specs=(P(None, "gx", "gy"), P(None, None, "gx", "gy")),
        check_vma=False,
    )
```

```python
import functools

import jax
import jax.numpy as jnp
from jax import lax
from jax.experimental import pallas as pl
from jax.experimental.pallas import tpu as pltpu
from jax.sharding import PartitionSpec as P

CX = 16
CY = 128
NZ = 8
SWEEPS = 4
MX = 2
MY = 16
HALO = 8
BLOCK = 4096
STAY = 64
LEAVE = 48

SCREENING = 0.5
CUBIC_TERM = 0.3
COUPLING = 1.5
SMOOTHING = 0.1
BACKGROUND = 1.0

MESH = pl.DeviceIdType.MESH
STEPS = ((1, 0), (-1, 0), (0, 1), (0, -1), (1, 1), (1, -1), (-1, 1), (-1, -1))


def deposit_kernel(
    counts_hbm, payload_hbm, cells_hbm, main, xs, ys, cs,
    stay_acc, leave_acc, counts, payload, cells, sems,
):
    part = payload.shape[1]
    copies = [
        pltpu.make_async_copy(counts_hbm, counts, sems.at[0]),
        pltpu.make_async_copy(cells_hbm, cells, sems.at[1]),
        pltpu.make_async_copy(payload_hbm, payload, sems.at[2]),
    ]
    for copy in copies:
        copy.start()
    stay_acc[...] = jnp.zeros_like(stay_acc)
    leave_acc[...] = jnp.zeros_like(leave_acc)
    bf16 = jnp.bfloat16
    base = lax.broadcasted_iota(jnp.int32, (16, 128), 0)
    ids = [(base + 16 * g).astype(jnp.float32).astype(bf16) for g in range(16)]
    ids = [jnp.concatenate([v] * (BLOCK // 128), axis=1) for v in ids]
    one = jnp.ones((16, BLOCK), bf16)
    none = jnp.zeros((16, BLOCK), bf16)
    for copy in copies:
        copy.wait()
    limits = []
    total = jnp.int32(0)
    for e in range(8):
        total = total + counts[0, e]
        limits.append(total)

    def packed(row):
        return jnp.broadcast_to(row.astype(jnp.float32), (16, BLOCK)).astype(bf16)

    def add(acc, count, span, row, col):
        col = packed(col)
        cols_hot = jnp.concatenate([jnp.where(v == col, one, none) for v in ids], axis=0)
        block = payload[:, span]
        first = lax.broadcasted_iota(jnp.int32, (4, BLOCK), 0) == 0
        values = block[0:1] * jnp.where(first, 1.0, block)
        high = values.astype(bf16).astype(jnp.float32)
        low = values - high
        wide = [packed(v[c : c + 1]) for v in (high, low) for c in range(4)]
        row = packed(row)
        masks = [ids[g] == row for g in range(count // 16)]
        left = jnp.concatenate([jnp.where(m, w, none) for w in wide for m in masks], axis=0)
        acc[...] += lax.dot_general(
            left, cols_hot, (((1,), (1,)), ((), ())), preferred_element_type=jnp.float32
        )

    def block_of(b):
        start = pl.multiple_of(b * BLOCK, BLOCK)
        span = pl.ds(start, BLOCK)
        position = start + lax.broadcasted_iota(jnp.int32, (1, BLOCK), 1)
        return span, position, cells[0:1, span], cells[1:2, span], cells[2:3, span]

    def stay_step(b, carry):
        span, position, k, i, j = block_of(b)
        row = jnp.where(position >= limits[7], k * 8 + (i & 7), 255)
        add(stay_acc, STAY, span, row, (i >> 3) * CY + j)
        return carry

    def leave_step(b, carry):
        span, position, k, i, j = block_of(b)
        direction = jnp.zeros((1, BLOCK), jnp.int32)
        for e in range(8):
            direction = direction + (position >= limits[e]).astype(jnp.int32)
        chunk = k * MY + (j & (MY - 1))
        layer = i & 1
        row = jnp.where(
            direction < 2, k * MX + layer, jnp.where(direction < 4, 16 + i, 28 + direction)
        )
        col = jnp.where(
            direction < 2,
            direction * CY + j,
            jnp.where(direction < 4, (direction - 2) * CY, layer * CY) + chunk,
        )
        row = jnp.where(direction == 8, 255, row)
        add(leave_acc, LEAVE, span, row, col)
        return carry

    blocks = part // BLOCK
    left_blocks = (limits[7] + (BLOCK - 1)) // BLOCK
    lax.fori_loop(0, left_blocks, leave_step, 0)
    lax.fori_loop(limits[7] // BLOCK, blocks, stay_step, 0)
    for c in range(4):
        for h in range(2):
            lanes = slice(h * CY, (h + 1) * CY)
            whole = (
                stay_acc[c * STAY : (c + 1) * STAY, lanes]
                + stay_acc[(4 + c) * STAY : (5 + c) * STAY, lanes]
            )
            main[c, :, 8 * h : 8 * h + 8, :] = whole.reshape(NZ, 8, CY)
            out = (
                leave_acc[c * LEAVE : (c + 1) * LEAVE, lanes]
                + leave_acc[(4 + c) * LEAVE : (5 + c) * LEAVE, lanes]
            )
            xs[h, c] = out[0:16]
            ys[h, c] = out[16:32]
            for d in range(4):
                cs[d, 2 * c + h : 2 * c + h + 1, :] = out[32 + d : 33 + d]


def relax_kernel(
    sizes, main, xs, ys, cs, field, momentum,
    rx, ry, rc, dens, edges, hx, hy, ext, src, u,
    send1, recv1, send2, recv2,
):
    n_gx, n_gy = sizes
    me_x = lax.axis_index("gx")
    me_y = lax.axis_index("gy")

    def device(step):
        return (lax.rem(me_x + step[0] + n_gx, n_gx), lax.rem(me_y + step[1] + n_gy, n_gy))

    barrier = pltpu.get_barrier_semaphore()
    for step in STEPS:
        pl.semaphore_signal(barrier, inc=1, device_id=device(step), device_id_type=MESH)
    pl.semaphore_wait(barrier, 8)

    def remote(src_ref, dst_ref, sems, recvs, d):
        return pltpu.make_async_remote_copy(
            src_ref=src_ref, dst_ref=dst_ref, send_sem=sems.at[d], recv_sem=recvs.at[d],
            device_id=device(STEPS[d]), device_id_type=MESH,
        )

    first = []
    for d in range(8):
        if d < 2:
            pair = (xs.at[d], rx.at[d])
        elif d < 4:
            pair = (ys.at[d - 2], ry.at[d - 2])
        else:
            pair = (cs.at[d - 4], rc.at[d - 4])
        first.append(remote(pair[0], pair[1], send1, recv1, d))
    for copy in first:
        copy.start()
    lane = lax.broadcasted_iota(jnp.int32, (1, CY), 1)
    lane16 = lax.broadcasted_iota(jnp.int32, (CX, CY), 1)
    for copy in first:
        copy.wait_recv()

    def collected(c):
        sides = []
        for s in range(2):
            low = rc[s, 2 * c : 2 * c + 2, :]
            high = rc[2 + s, 2 * c : 2 * c + 2, :]
            pad = jnp.zeros((CX - 2 * MX, CY), jnp.float32)
            sides.append(ry[s, c] + jnp.concatenate([low, pad, high], axis=0))
        pad = jnp.zeros((CX - 2 * MX, CY), jnp.float32)
        out = []
        for k in range(NZ):
            left = pltpu.roll(sides[0], (CY - MY * k) % CY, axis=1)
            right = pltpu.roll(sides[1], (2 * CY - MY - MY * k) % CY, axis=1)
            extra = jnp.where(lane16 < MY, left, jnp.where(lane16 >= CY - MY, right, 0.0))
            faces = jnp.concatenate(
                [rx[0, c, 2 * k : 2 * k + 2, :], pad, rx[1, c, 2 * k : 2 * k + 2, :]], axis=0
            )
            out.append(main[c, k] + faces + extra)
        return out

    rho = collected(0)
    low_edge = jnp.zeros((CX, CY), jnp.float32)
    high_edge = jnp.zeros((CX, CY), jnp.float32)
    for k in range(NZ):
        dens[k] = rho[k]
        here = (lane16 >= MY * k) & (lane16 < MY * (k + 1))
        low_edge = jnp.where(here, pltpu.roll(rho[k], MY * k, axis=1), low_edge)
        high_edge = jnp.where(here, pltpu.roll(rho[k], (MY * (k + 1)) % CY, axis=1), high_edge)
    edges[0] = low_edge
    edges[1] = high_edge

    second = [
        (dens.at[:, 8:16, :], hx.at[0]),
        (dens.at[:, 0:8, :], hx.at[1]),
        (edges.at[1], hy.at[1, 8:24, :]),
        (edges.at[0], hy.at[0, 8:24, :]),
        (edges.at[1, 8:16, :], hy.at[1, 0:8, :]),
        (edges.at[0, 8:16, :], hy.at[0, 0:8, :]),
        (edges.at[1, 0:8, :], hy.at[1, 24:32, :]),
        (edges.at[0, 0:8, :], hy.at[0, 24:32, :]),
    ]
    second = [remote(a, b, send2, recv2, d) for d, (a, b) in enumerate(second)]
    for copy in second:
        copy.start()
    for c in range(1, 4):
        for k, layer in enumerate(collected(c)):
            momentum[c - 1, k] = layer
    for copy in second:
        copy.wait_recv()

    lane32 = lax.broadcasted_iota(jnp.int32, (32, CY), 1)
    for k in range(NZ):
        ext[k, 0:8, 0:CY] = hx[0, k]
        ext[k, 8:24, 0:CY] = dens[k]
        ext[k, 24:32, 0:CY] = hx[1, k]
        after = pltpu.roll(hy[0], (CY - MY * k) % CY, axis=1)
        before = pltpu.roll(hy[1], (2 * CY - MY - MY * k) % CY, axis=1)
        ext[k, :, CY:] = jnp.where(
            lane32 < MY, after, jnp.where(lane32 >= CY - MY, before, 0.0)
        )

    def around(ref, k):
        mid = ref[k]
        total = (
            pltpu.roll(mid, 1, axis=0)
            + pltpu.roll(mid, 31, axis=0)
            + pltpu.roll(mid, 1, axis=1)
            + pltpu.roll(mid, 2 * CY - 1, axis=1)
        )
        if k > 0:
            total = total + ref[k - 1]
        if k < NZ - 1:
            total = total + ref[k + 1]
        return mid, total

    odd = (
        lax.broadcasted_iota(jnp.int32, (32, 2 * CY), 0)
        + lax.broadcasted_iota(jnp.int32, (32, 2 * CY), 1)
    ) & 1
    for k in range(NZ):
        mid, near = around(ext, k)
        value = COUPLING * (mid + SMOOTHING * (near - 6.0 * mid) - BACKGROUND)
        src[k] = value
        u[k] = jnp.where(odd == (k & 1), value * (-1.0 / (6.0 + SCREENING)), 0.0)

    def relaxed(mid, near, source):
        square = mid * mid
        slope = (6.0 + SCREENING) + (3.0 * CUBIC_TERM) * square
        r = near - source - mid * ((6.0 + SCREENING) + CUBIC_TERM * square)
        inverse = pl.reciprocal(slope, approx=True)
        inverse = inverse * (2.0 - slope * inverse)
        return mid + r * inverse

    def half(colour):
        for k in range(NZ):
            mid, near = around(u, k)
            new = relaxed(mid, near, src[k])
            u[k] = jnp.where(odd == ((k + colour) & 1), new, mid)

    def sweep(n, carry):
        half(1)
        half(0)
        return carry

    lax.fori_loop(0, SWEEPS - 1, sweep, 0)
    odd_tile = odd[8:24, 0:CY]
    for k in range(NZ):
        wide = u[k, 8:24, :]
        mid = wide[:, 0:CY]
        near = (
            u[k, 7:23, 0:CY]
            + u[k, 9:25, 0:CY]
            + pltpu.roll(wide, 1, axis=1)[:, 0:CY]
            + pltpu.roll(wide, 2 * CY - 1, axis=1)[:, 0:CY]
        )
        if k > 0:
            near = near + u[k - 1, 8:24, 0:CY]
        if k < NZ - 1:
            near = near + u[k + 1, 8:24, 0:CY]
        new = relaxed(mid, near, src[k, 8:24, 0:CY])
        field[k] = jnp.where(odd_tile == ((k + 1) & 1), new, mid)
    for copy in first + second:
        copy.wait_send()


def shards(sizes, payload, cells, counts):
    f32 = jnp.float32
    vmem = pl.BlockSpec(memory_space=pltpu.VMEM)
    main, xs, ys, cs = pl.pallas_call(
        deposit_kernel,
        out_shape=(
            jax.ShapeDtypeStruct((4, NZ, CX, CY), f32),
            jax.ShapeDtypeStruct((2, 4, NZ * MX, CY), f32),
            jax.ShapeDtypeStruct((2, 4, CX, CY), f32),
            jax.ShapeDtypeStruct((4, 8, CY), f32),
        ),
        in_specs=[pl.BlockSpec(memory_space=pltpu.HBM)] * 3,
        out_specs=(vmem,) * 4,
        scratch_shapes=[
            pltpu.VMEM((8 * STAY, 2 * CY), f32),
            pltpu.VMEM((8 * LEAVE, 2 * CY), f32),
            pltpu.SMEM(counts.shape, jnp.int32),
            pltpu.VMEM(payload.shape, f32),
            pltpu.VMEM(cells.shape, jnp.int32),
            pltpu.SemaphoreType.DMA((3,)),
        ],
        compiler_params=pltpu.CompilerParams(vmem_limit_bytes=40 * 1024 * 1024),
        name="deposit",
    )(*[pltpu.with_memory_space_constraint(a, pltpu.HBM) for a in (counts, payload, cells)])
    field, momentum = pl.pallas_call(
        functools.partial(relax_kernel, sizes),
        out_shape=(
            jax.ShapeDtypeStruct((NZ, CX, CY), f32),
            jax.ShapeDtypeStruct((3, NZ, CX, CY), f32),
        ),
        in_specs=[vmem] * 4,
        out_specs=(vmem,) * 2,
        scratch_shapes=[
            pltpu.VMEM((2, 4, NZ * MX, CY), f32),
            pltpu.VMEM((2, 4, CX, CY), f32),
            pltpu.VMEM((4, 8, CY), f32),
            pltpu.VMEM((NZ, CX, CY), f32),
            pltpu.VMEM((2, CX, CY), f32),
            pltpu.VMEM((2, NZ, 8, CY), f32),
            pltpu.VMEM((2, 32, CY), f32),
            pltpu.VMEM((NZ, 32, 2 * CY), f32),
            pltpu.VMEM((NZ, 32, 2 * CY), f32),
            pltpu.VMEM((NZ, 32, 2 * CY), f32),
        ] + [pltpu.SemaphoreType.DMA((8,))] * 4,
        compiler_params=pltpu.CompilerParams(
            collective_id=0, has_side_effects=True, vmem_limit_bytes=40 * 1024 * 1024
        ),
        name="relax",
    )(main, xs, ys, cs)
    return field, momentum


def solution(mesh):
    sizes = (mesh.shape["gx"], mesh.shape["gy"])
    placed = (P(None, ("gx", "gy")), P(None, ("gx", "gy")), P(("gx", "gy"), None))
    return jax.shard_map(
        functools.partial(shards, sizes),
        mesh=mesh,
        in_specs=placed,
        out_specs=(P(None, "gx", "gy"), P(None, None, "gx", "gy")),
        check_vma=False,
    )
```
